32 devices in a mesh: frames: 8 (over y, x, core), rows: 4 (over z).
Axes of the slice: x: 2, y: 2, z: 4, core: 2. Of those that a mesh axis runs over, the one named last changes fastest.
Arguments:
- clip: bfloat16 [16, 32, 512, 256], P('frames', 'rows'), may hold values from -6 to 6
- w_query: bfloat16 [256, 256], replicated, may hold values from -32 to 32
- w_key: bfloat16 [256, 256], replicated, may hold values from -1 to 1
- w_value: bfloat16 [256, 256], replicated, may hold values from -0.375 to 0.375
- w_out: bfloat16 [256, 256], replicated, may hold values from -0.375 to 0.375
- w_conv: bfloat16 [3, 3, 256, 256], replicated, may hold values from -0.125 to 0.125
- conv_bias: float32 [256], replicated, may hold values from -3 to 3
Outputs:
- upsampled: bfloat16 [16, 64, 512, 128], P('frames', 'rows')
The draws below stay inside these ranges and needn't reach their ends.
All inputs are finite; a program needn't handle non-finite values.
Results may differ from the reference program's by a relative error of at most 0.012.
Values may be sent and summed in bfloat16 or wider, within the bound.
A program may use at most 192 MiB of HBM per device.

```python
import math
import jax
import jax.numpy as jnp
from jax import lax

C = 256
HEADS = 8
HD = 32
CO = 64
W = 512
FRAMES = 16
H = 32


def key_matrix(key):
    return jax.random.normal(key, (C, C), jnp.float32) / math.sqrt(C)


def draw_w_key(key, part):
    return jnp.clip(key_matrix(key), -1.0, 1.0).astype(jnp.bfloat16)


def draw_w_query(key, part):
    key = jax.random.fold_in(key, 7)
    own = jnp.clip(jax.random.normal(key, (C, C), jnp.float32) / math.sqrt(C), -1.0, 1.0)
    matrix = own
    return matrix.astype(jnp.bfloat16)


def draw_clip(key, part):
    key = jax.random.fold_in(key, 11)
    values = jax.random.normal(key, (FRAMES, H, W, C), jnp.float32)
    return jnp.clip(values, -6.0, 6.0).astype(jnp.bfloat16)


def scatter_about(stream_key, extent, scale, reach, held_as=jnp.bfloat16):
    values = scale * jax.random.normal(stream_key, extent, jnp.float32)
    return jnp.clip(values, min=-reach, max=reach).astype(held_as)


def setup_inputs(seed: int = 0) -> dict:
    seeds = jax.random.split(jax.random.key(seed), 8)
    clip = draw_clip(jax.random.fold_in(seeds[7], 71), 0)
    w_query = draw_w_query(jax.random.fold_in(seeds[7], 71), 0)
    w_key = draw_w_key(jax.random.fold_in(seeds[7], 71), 0)
    w_value = scatter_about(seeds[3], (C, C), C ** -0.5, 0.375)
    w_out = scatter_about(seeds[4], (C, C), C ** -0.5, 0.375)
    w_conv = scatter_about(seeds[5], (3, 3, C, C), (9 * C) ** -0.5, 0.125)
    conv_bias = scatter_about(seeds[6], (C,), 0.5, 3.0, jnp.float32)
    return {"clip": clip, "w_query": w_query, "w_key": w_key, "w_value": w_value, "w_out": w_out, "w_conv": w_conv, "conv_bias": conv_bias}


def normalize(x):
    values = x.astype(jnp.float32)
    mean = lax.optimization_barrier(jnp.mean(values, axis=-1, keepdims=True))
    centred = values - mean
    var = lax.optimization_barrier(jnp.mean(centred * centred, axis=-1, keepdims=True))
    return (centred * lax.rsqrt(var + 1e-06)).astype(jnp.bfloat16)

def project(x, weight):
    shape = x.shape
    out = jnp.dot(x.reshape(-1, shape[-1]), weight, preferred_element_type=jnp.float32)
    return out.astype(jnp.bfloat16).reshape(shape[:-1] + (weight.shape[1],))

def one_row(row, w_query, w_key, w_value, w_out):
    frames_all, width, chans = row.shape
    normed = normalize(row)
    query = project(normed, w_query).reshape(frames_all, width, HEADS, HD)
    keys = project(normed, w_key).reshape(frames_all, width, HEADS, HD)
    values = project(normed, w_value).reshape(frames_all, width, HEADS, HD)
    scores = jnp.einsum('fphd,gphd->phfg', query.astype(jnp.float32), keys.astype(jnp.float32)) / jnp.sqrt(jnp.float32(HD))
    probs = jax.nn.softmax(scores, axis=-1).astype(jnp.bfloat16)
    attended = jnp.einsum('phfg,gphd->fphd', probs.astype(jnp.float32), values.astype(jnp.float32)).astype(jnp.bfloat16)
    return project(attended.reshape(frames_all, width, chans), w_out)

def reference(clip, w_query, w_key, w_value, w_out, w_conv, conv_bias):
    by_rows = jnp.moveaxis(clip, 1, 0)
    projected = lax.map(lambda row: one_row(row, w_query, w_key, w_value, w_out), by_rows)
    projected = jnp.moveaxis(projected, 0, 1)
    hidden = clip.astype(jnp.float32) + projected.astype(jnp.float32)
    activated = jax.nn.silu(hidden).astype(jnp.bfloat16)
    convolved = lax.conv_general_dilated(activated, w_conv, (1, 1), ((1, 1), (1, 1)), dimension_numbers=('NHWC', 'HWIO', 'NHWC'), preferred_element_type=jnp.float32)
    mixed = (hidden + convolved + conv_bias).astype(jnp.bfloat16)
    frames_all, height, width, chans = mixed.shape
    split = mixed.reshape(frames_all, height, width, 2, 2 * CO)
    return jnp.transpose(split, (0, 1, 3, 2, 4)).reshape(frames_all, 2 * height, width, 2 * CO)
```

```python
import functools
import math

import jax
import jax.numpy as jnp
from jax import lax
from jax.experimental import pallas as pl
from jax.experimental.pallas import tpu as pltpu
from jax.sharding import PartitionSpec as P

HEADS = 8
PAIRS = HEADS // 2
MESH = pl.DeviceIdType.MESH
NT = (((1,), (1,)), ((), ()))


def attend_block(x, wqv_t, wk, wo):
    frames, _, chans = x.shape
    n = frames * 8
    hd = chans // HEADS
    x = x.astype(jnp.float32)
    mean = jnp.mean(x, axis=-1, keepdims=True)
    centred = x - mean
    var = jnp.mean(centred * centred, axis=-1, keepdims=True)
    xn = centred * lax.rsqrt(var + 1e-6)
    xs = jnp.concatenate(
        [xn[:, :8].reshape(n, chans), xn[:, 8:].reshape(n, chans)], axis=0
    ).astype(jnp.bfloat16)
    qv = lax.dot_general(wqv_t, xs, NT, preferred_element_type=jnp.float32).astype(jnp.bfloat16)
    keys = jnp.dot(xs, wk, preferred_element_type=jnp.float32).astype(jnp.bfloat16)

    head_row = lax.broadcasted_iota(jnp.int32, (chans, n), 0) // hd
    even = (head_row % 2 == 0).astype(jnp.float32).astype(jnp.bfloat16)
    odd = (head_row % 2 == 1).astype(jnp.float32).astype(jnp.bfloat16)
    pair_col = lax.broadcasted_iota(jnp.int32, (n, chans), 1) // (2 * hd)
    own = lax.broadcasted_iota(jnp.int32, (8, 2 * n), 0) == (
        lax.broadcasted_iota(jnp.int32, (8, 2 * n), 1) % 8
    )
    scale = math.log2(math.e) / math.sqrt(hd)

    attended = []
    for g in range(2):
        cols = slice(g * n, (g + 1) * n)
        q_t, v_t, k = qv[:chans, cols], qv[chans:, cols], keys[cols]
        rhs = jnp.concatenate([q_t * even, q_t * odd], axis=1)
        lhs = jnp.concatenate(
            [
                k * (pair_col == j).astype(jnp.float32).astype(jnp.bfloat16)
                for j in range(PAIRS)
            ],
            axis=0,
        )
        s = jnp.dot(lhs, rhs, preferred_element_type=jnp.float32)
        pieces = []
        for j in range(PAIRS):
            sj = s[j * n:(j + 1) * n].reshape(frames, 8, 2 * n)
            top = jnp.max(sj, axis=0, keepdims=True)
            e = jnp.exp2((sj - top) * scale)
            total = jnp.sum(e, axis=0)
            inv = jnp.where(own, 1.0 / total, 0.0)
            p = (e * inv[None]).reshape(n, 2 * n).astype(jnp.bfloat16)
            o = jnp.dot(v_t[2 * hd * j:2 * hd * (j + 1)], p, preferred_element_type=jnp.float32)
            pieces += [o[:hd, :n], o[hd:, n:]]
        attended.append(jnp.concatenate(pieces, axis=0).T)
    attended = jnp.concatenate(attended, axis=0).astype(jnp.bfloat16)
    out = jnp.dot(attended, wo, preferred_element_type=jnp.float32)
    return jnp.concatenate(
        [out[:n].reshape(frames, 8, chans), out[n:].reshape(frames, 8, chans)], axis=1
    ).astype(jnp.bfloat16)


def kernel(
    sizes, clip, wq, wk, wv, wo, wc, bias, out,
    clipv, xr, pr, back, act, stage, wqv_t,
    clip_sem, f_send, f_recv, b_send, b_recv, h_send, h_recv, o_sem,
):
    n_dev, n_strip, fl, rows, width, chans = sizes
    pw = width // n_dev
    me = lax.axis_index("frames")
    strip = lax.axis_index("rows")
    mine = pl.multiple_of(me * pw, pw)

    def peer(k):
        return lax.rem(me + k, n_dev)

    def forward(r, k):
        to = peer(k)
        return pltpu.make_async_remote_copy(
            src_ref=clip.at[:, r, pl.ds(pl.multiple_of(to * pw, pw), pw), :],
            dst_ref=xr.at[r, pl.ds(me * fl, fl)],
            send_sem=f_send.at[r, k],
            recv_sem=f_recv.at[r, k],
            device_id={"frames": to},
            device_id_type=MESH,
        )

    def forward_own(r):
        return pltpu.make_async_copy(
            clip.at[:, r, pl.ds(mine, pw), :], xr.at[r, pl.ds(me * fl, fl)], f_recv.at[r, 0]
        )

    def backward(r, k):
        to = peer(k)
        return pltpu.make_async_remote_copy(
            src_ref=pr.at[r, pl.ds(to * fl, fl)],
            dst_ref=back.at[r, :, pl.ds(mine, pw), :],
            send_sem=b_send.at[r, k],
            recv_sem=b_recv.at[r, k],
            device_id={"frames": to},
            device_id_type=MESH,
        )

    def backward_own(r):
        return pltpu.make_async_copy(
            pr.at[r, pl.ds(me * fl, fl)], back.at[r, :, pl.ds(mine, pw), :], b_recv.at[r, 0]
        )

    def halo(down):
        src, dst = (rows, 0) if down else (1, rows + 1)
        return pltpu.make_async_remote_copy(
            src_ref=act.at[src, :, :, pl.ds(chans, chans)],
            dst_ref=act.at[dst, :, :, pl.ds(chans, chans)],
            send_sem=h_send.at[int(down)],
            recv_sem=h_recv.at[int(down)],
            device_id={"rows": strip + 1 if down else strip - 1},
            device_id_type=MESH,
        )

    def order(i):
        return jnp.where(i == 0, 0, jnp.where(i == 1, rows - 1, i - 1))

    has_prev, has_next = strip > 0, strip < n_strip - 1

    barrier = pltpu.get_barrier_semaphore()

    @pl.loop(1, n_dev)
    def _(k):
        pl.semaphore_signal(barrier, inc=1, device_id={"frames": peer(k)}, device_id_type=MESH)

    @pl.when(has_prev)
    def _():
        pl.semaphore_signal(barrier, inc=1, device_id={"rows": strip - 1}, device_id_type=MESH)

    @pl.when(has_next)
    def _():
        pl.semaphore_signal(barrier, inc=1, device_id={"rows": strip + 1}, device_id_type=MESH)

    @pl.loop(0, rows)
    def _(i):
        forward_own(order(i)).start()

    pl.semaphore_wait(
        barrier, n_dev - 1 + has_prev.astype(jnp.int32) + has_next.astype(jnp.int32)
    )

    @pl.loop(0, rows)
    def _(i):
        @pl.loop(1, n_dev)
        def _(k):
            forward(order(i), k).start()

    whole = pltpu.make_async_copy(clip, clipv, clip_sem)
    whole.start()
    wqv_t[:chans] = wq[...].astype(jnp.float32).T.astype(jnp.bfloat16)
    wqv_t[chans:] = wv[...].astype(jnp.float32).T.astype(jnp.bfloat16)

    @pl.loop(0, rows)
    def _(i):
        r = order(i)
        forward_own(r).wait()

        @pl.loop(1, n_dev)
        def _(k):
            forward(r, k).wait_recv()

        @pl.loop(0, pw // 16)
        def _(b):
            at = pl.ds(pl.multiple_of(b * 16, 16), 16)
            pr[r, :, at, :] = attend_block(xr[r, :, at, :], wqv_t[...], wk[...], wo[...])

        @pl.loop(1, n_dev)
        def _(k):
            backward(r, k).start()

        backward_own(r).start()

    whole.wait()

    def spread(a, row, f):
        pixel = lax.broadcasted_iota(jnp.int32, a.shape, 0)
        before = jnp.where(pixel == 0, 0.0, pltpu.roll(a, 1, 0))
        after = jnp.where(pixel == width - 1, 0.0, pltpu.roll(a, width - 1, 0))
        act[row, f, :, pl.ds(0, chans)] = before.astype(jnp.bfloat16)
        act[row, f, :, pl.ds(2 * chans, chans)] = after.astype(jnp.bfloat16)

    def activate(r):
        backward_own(r).wait()

        @pl.loop(1, n_dev)
        def _(k):
            backward(r, k).wait_recv()

        @pl.loop(0, fl)
        def _(f):
            h = clipv[f, r].astype(jnp.float32) + back[r, f].astype(jnp.float32)
            half = 0.5 * h
            a = half + half * jnp.tanh(half)
            act[r + 1, f, :, pl.ds(chans, chans)] = a.astype(jnp.bfloat16)
            spread(a, r + 1, f)

    def out_copy(r):
        return pltpu.make_async_copy(
            stage.at[:, pl.ds(2 * r, 2)], out.at[:, pl.ds(2 * r, 2)], o_sem.at[r]
        )

    def convolve(r):
        tile = min(width, 256)

        @pl.loop(0, fl)
        def _(f):
            @pl.loop(0, width // tile)
            def _(t):
                at = pl.ds(pl.multiple_of(t * tile, tile), tile)
                total = clipv[f, r, at, :].astype(jnp.float32) + back[r, f, at, :].astype(jnp.float32)
                total = total + bias[...]
                for d in range(3):
                    total = total + jnp.dot(
                        act[r + d, f, at, :], wc[d], preferred_element_type=jnp.float32
                    )
                mixed = total.astype(jnp.bfloat16)
                stage[f, 2 * r, at, :] = mixed[:, :chans // 2]
                stage[f, 2 * r + 1, at, :] = mixed[:, chans // 2:]

        out_copy(r).start()

    @pl.loop(0, 2)
    def _(i):
        activate(i * (rows - 1))

    @pl.when(has_prev)
    def _():
        halo(False).start()

    @pl.when(has_next)
    def _():
        halo(True).start()

    activate(1)

    @pl.loop(1, rows - 2)
    def _(r):
        activate(r + 1)
        convolve(r)

    def spread_halo(row):
        @pl.loop(0, fl)
        def _(f):
            spread(act[row, f, :, pl.ds(chans, chans)].astype(jnp.float32), row, f)

    def clear(row):
        act[row] = jnp.zeros(act.shape[1:], act.dtype)

    @pl.when(has_prev)
    def _():
        halo(True).wait_recv()
        spread_halo(0)

    @pl.when(jnp.logical_not(has_prev))
    def _():
        clear(0)

    @pl.when(has_next)
    def _():
        halo(False).wait_recv()
        spread_halo(rows + 1)

    @pl.when(jnp.logical_not(has_next))
    def _():
        clear(rows + 1)

    @pl.loop(0, 3)
    def _(i):
        convolve(lax.rem(i + rows - 2, rows))

    @pl.loop(0, rows)
    def _(r):
        @pl.loop(1, n_dev)
        def _(k):
            forward(r, k).wait_send()
            backward(r, k).wait_send()

        out_copy(r).wait()

    @pl.when(has_prev)
    def _():
        halo(False).wait_send()

    @pl.when(has_next)
    def _():
        halo(True).wait_send()


def local(n_dev, n_strip, clip, w_query, w_key, w_value, w_out, w_conv, conv_bias):
    fl, rows, width, chans = clip.shape
    frames = fl * n_dev
    pw = width // n_dev
    sizes = (n_dev, n_strip, fl, rows, width, chans)
    bf16 = jnp.bfloat16
    vmem = pl.BlockSpec(memory_space=pltpu.VMEM)
    hbm = pl.BlockSpec(memory_space=pl.ANY)
    positions = fl * rows * width
    return pl.pallas_call(
        functools.partial(kernel, sizes),
        out_shape=jax.ShapeDtypeStruct((fl, 2 * rows, width, chans // 2), bf16),
        in_specs=[hbm] + [vmem] * 6,
        out_specs=hbm,
        scratch_shapes=[
            pltpu.VMEM((fl, rows, width, chans), bf16),
            pltpu.VMEM((rows, frames, pw, chans), bf16),
            pltpu.VMEM((rows, frames, pw, chans), bf16),
            pltpu.VMEM((rows, fl, width, chans), bf16),
            pltpu.VMEM((rows + 2, fl, width, 3 * chans), bf16),
            pltpu.VMEM((fl, 2 * rows, width, chans // 2), bf16),
            pltpu.VMEM((2 * chans, chans), bf16),
            pltpu.SemaphoreType.DMA,
            pltpu.SemaphoreType.DMA((rows, n_dev)),
            pltpu.SemaphoreType.DMA((rows, n_dev)),
            pltpu.SemaphoreType.DMA((rows, n_dev)),
            pltpu.SemaphoreType.DMA((rows, n_dev)),
            pltpu.SemaphoreType.DMA((2,)),
            pltpu.SemaphoreType.DMA((2,)),
            pltpu.SemaphoreType.DMA((rows,)),
        ],
        compiler_params=pltpu.CompilerParams(
            collective_id=0, has_side_effects=True, vmem_limit_bytes=58 * 1024 * 1024
        ),
        cost_estimate=pl.CostEstimate(
            flops=positions * chans * chans * 2 * 13,
            bytes_accessed=positions * chans * 2 * 4,
            transcendentals=positions * chans * 8,
        ),
    )(
        clip, w_query, w_key, w_value, w_out,
        w_conv.reshape(3, 3 * chans, chans), conv_bias.reshape(1, chans),
    )


def solution(mesh):
    placed = (P("frames", "rows", None, None), P(), P(), P(), P(), P(), P())
    return jax.shard_map(
        functools.partial(local, mesh.shape["frames"], mesh.shape["rows"]),
        mesh=mesh,
        in_specs=placed,
        out_specs=P("frames", "rows", None, None),
        check_vma=False,
    )
```

```python
import functools
import math

import jax
import jax.numpy as jnp
from jax import lax
from jax.experimental import pallas as pl
from jax.experimental.pallas import tpu as pltpu
from jax.sharding import PartitionSpec as P

HEADS = 8
PAIRS = HEADS // 2
LAG = 4
MESH = pl.DeviceIdType.MESH
NT = (((1,), (1,)), ((), ()))


def attend_block(x, wqv_t, wk, wo):
    frames, _, chans = x.shape
    n = frames * 8
    hd = chans // HEADS
    x = x.astype(jnp.float32)
    mean = jnp.mean(x, axis=-1, keepdims=True)
    centred = x - mean
    var = jnp.mean(centred * centred, axis=-1, keepdims=True)
    xn = centred * lax.rsqrt(var + 1e-6)
    xs = jnp.concatenate(
        [xn[:, :8].reshape(n, chans), xn[:, 8:].reshape(n, chans)], axis=0
    ).astype(jnp.bfloat16)
    qv = lax.dot_general(wqv_t, xs, NT, preferred_element_type=jnp.float32).astype(jnp.bfloat16)
    keys = jnp.dot(xs, wk, preferred_element_type=jnp.float32).astype(jnp.bfloat16)

    head_row = lax.broadcasted_iota(jnp.int32, (chans, n), 0) // hd
    even = (head_row % 2 == 0).astype(jnp.float32).astype(jnp.bfloat16)
    odd = (head_row % 2 == 1).astype(jnp.float32).astype(jnp.bfloat16)
    pair_col = lax.broadcasted_iota(jnp.int32, (n, chans), 1) // (2 * hd)
    own = lax.broadcasted_iota(jnp.int32, (8, 2 * n), 0) == (
        lax.broadcasted_iota(jnp.int32, (8, 2 * n), 1) % 8
    )
    scale = math.log2(math.e) / math.sqrt(hd)

    attended = []
    for g in range(2):
        cols = slice(g * n, (g + 1) * n)
        q_t, v_t, k = qv[:chans, cols], qv[chans:, cols], keys[cols]
        rhs = jnp.concatenate([q_t * even, q_t * odd], axis=1)
        lhs = jnp.concatenate(
            [
                k * (pair_col == j).astype(jnp.float32).astype(jnp.bfloat16)
                for j in range(PAIRS)
            ],
            axis=0,
        )
        s = jnp.dot(lhs, rhs, preferred_element_type=jnp.float32)
        pieces = []
        for j in range(PAIRS):
            sj = s[j * n:(j + 1) * n].reshape(frames, 8, 2 * n)
            top = jnp.max(sj, axis=0, keepdims=True)
            e = jnp.exp2((sj - top) * scale)
            total = jnp.sum(e, axis=0)
            inv = jnp.where(own, 1.0 / total, 0.0)
            p = (e * inv[None]).reshape(n, 2 * n).astype(jnp.bfloat16)
            o = jnp.dot(v_t[2 * hd * j:2 * hd * (j + 1)], p, preferred_element_type=jnp.float32)
            pieces += [o[:hd, :n], o[hd:, n:]]
        attended.append(jnp.concatenate(pieces, axis=0).T)
    attended = jnp.concatenate(attended, axis=0).astype(jnp.bfloat16)
    out = jnp.dot(attended, wo, preferred_element_type=jnp.float32)
    return jnp.concatenate(
        [out[:n].reshape(frames, 8, chans), out[n:].reshape(frames, 8, chans)], axis=1
    ).astype(jnp.bfloat16)


def offsets(n_dev):
    chips = list(range(1, n_dev // 2))
    swapped = list(chips)
    for i in range(0, len(chips) - 1, 2):
        swapped[i], swapped[i + 1] = chips[i + 1], chips[i]
    return [[2 * chip + half for half in range(2) for chip in c] + [1] for c in (chips, swapped)]


def kernel(
    sizes, clip, wq, wk, wv, wo, wc, bias, out,
    clipv, xr, pr, back, act, wqv_t,
    clip_sem, f_send, f_recv, b_send, b_recv, h_send, h_recv,
):
    n_dev, n_strip, fl, rows, width, chans = sizes
    pw = width // n_dev
    me = lax.axis_index("frames")
    strip = lax.axis_index("rows")
    mine = pl.multiple_of(me * pw, pw)

    def peer(k):
        out = 0
        for bit in range(n_dev.bit_length() - 1):
            one = 1 << bit
            out = out + lax.rem(lax.div(me, one) + lax.div(k, one), 2) * one
        return out

    def start_to_all(copy, r):
        core = lax.rem(me, 2)
        for a, b in zip(*offsets(n_dev)):
            copy(r, jnp.where(core == 0, a, b)).start()

    def forward(r, k):
        to = peer(k)
        return pltpu.make_async_remote_copy(
            src_ref=clip.at[:, r, pl.ds(pl.multiple_of(to * pw, pw), pw), :],
            dst_ref=xr.at[r, pl.ds(me * fl, fl)],
            send_sem=f_send.at[r, k],
            recv_sem=f_recv.at[r, k],
            device_id={"frames": to},
            device_id_type=MESH,
        )

    def forward_own(r):
        return pltpu.make_async_copy(
            clip.at[:, r, pl.ds(mine, pw), :], xr.at[r, pl.ds(me * fl, fl)], f_recv.at[r, 0]
        )

    def backward(r, k):
        to = peer(k)
        return pltpu.make_async_remote_copy(
            src_ref=pr.at[r, pl.ds(to * fl, fl)],
            dst_ref=back.at[r, :, pl.ds(mine, pw), :],
            send_sem=b_send.at[r, k],
            recv_sem=b_recv.at[r, k],
            device_id={"frames": to},
            device_id_type=MESH,
        )

    def backward_own(r):
        return pltpu.make_async_copy(
            pr.at[r, pl.ds(me * fl, fl)], back.at[r, :, pl.ds(mine, pw), :], b_recv.at[r, 0]
        )

    def halo(down):
        src, dst = (rows, 0) if down else (1, rows + 1)
        return pltpu.make_async_remote_copy(
            src_ref=act.at[src, :, :, pl.ds(chans, chans)],
            dst_ref=act.at[dst, :, :, pl.ds(chans, chans)],
            send_sem=h_send.at[int(down)],
            recv_sem=h_recv.at[int(down)],
            device_id={"rows": strip + 1 if down else strip - 1},
            device_id_type=MESH,
        )

    def order(i):
        return jnp.where(i == 0, 0, jnp.where(i == 1, rows - 1, i - 1))

    has_prev, has_next = strip > 0, strip < n_strip - 1

    barrier = pltpu.get_barrier_semaphore()

    @pl.loop(1, n_dev)
    def _(k):
        pl.semaphore_signal(barrier, inc=1, device_id={"frames": peer(k)}, device_id_type=MESH)

    @pl.when(has_prev)
    def _():
        pl.semaphore_signal(barrier, inc=1, device_id={"rows": strip - 1}, device_id_type=MESH)

    @pl.when(has_next)
    def _():
        pl.semaphore_signal(barrier, inc=1, device_id={"rows": strip + 1}, device_id_type=MESH)

    @pl.loop(0, rows)
    def _(i):
        forward_own(order(i)).start()

    pl.semaphore_wait(
        barrier, n_dev - 1 + has_prev.astype(jnp.int32) + has_next.astype(jnp.int32)
    )

    @pl.loop(0, rows)
    def _(i):
        start_to_all(forward, order(i))

    whole = pltpu.make_async_copy(clip, clipv, clip_sem)
    whole.start()
    wqv_t[:chans] = wq[...].astype(jnp.float32).T.astype(jnp.bfloat16)
    wqv_t[chans:] = wv[...].astype(jnp.float32).T.astype(jnp.bfloat16)

    def attend(r):
        forward_own(r).wait()

        @pl.loop(1, n_dev)
        def _(k):
            forward(r, k).wait_recv()

        @pl.loop(0, pw // 16)
        def _(b):
            at = pl.ds(pl.multiple_of(b * 16, 16), 16)
            pr[r, :, at, :] = attend_block(xr[r, :, at, :], wqv_t[...], wk[...], wo[...])

        start_to_all(backward, r)
        backward_own(r).start()

    def spread(a, row, f):
        pixel = lax.broadcasted_iota(jnp.int32, a.shape, 0)
        before = jnp.where(pixel == 0, 0.0, pltpu.roll(a, 1, 0))
        after = jnp.where(pixel == width - 1, 0.0, pltpu.roll(a, width - 1, 0))
        act[row, f, :, pl.ds(0, chans)] = before.astype(jnp.bfloat16)
        act[row, f, :, pl.ds(2 * chans, chans)] = after.astype(jnp.bfloat16)

    def activate(r):
        backward_own(r).wait()

        @pl.loop(1, n_dev)
        def _(k):
            backward(r, k).wait_recv()

        @pl.loop(0, fl)
        def _(f):
            h = clipv[f, r].astype(jnp.float32) + back[r, f].astype(jnp.float32)
            half = 0.5 * h
            a = half + half * jnp.tanh(half)
            act[r + 1, f, :, pl.ds(chans, chans)] = a.astype(jnp.bfloat16)
            spread(a, r + 1, f)

    def convolve(r):
        tile = min(width, 256)

        @pl.loop(0, fl)
        def _(f):
            @pl.loop(0, width // tile)
            def _(t):
                at = pl.ds(pl.multiple_of(t * tile, tile), tile)
                total = clipv[f, r, at, :].astype(jnp.float32) + back[r, f, at, :].astype(jnp.float32)
                total = total + bias[...]
                for d in range(3):
                    total = total + jnp.dot(
                        act[r + d, f, at, :], wc[d], preferred_element_type=jnp.float32
                    )
                mixed = total.astype(jnp.bfloat16)
                out[f, 2 * r, at, :] = mixed[:, :chans // 2]
                out[f, 2 * r + 1, at, :] = mixed[:, chans // 2:]

    def spread_halo(row):
        @pl.loop(0, fl)
        def _(f):
            spread(act[row, f, :, pl.ds(chans, chans)].astype(jnp.float32), row, f)

    def clear(row):
        act[row] = jnp.zeros(act.shape[1:], act.dtype)

    def finish_halo():
        @pl.when(has_prev)
        def _():
            halo(True).wait_recv()
            spread_halo(0)

        @pl.when(jnp.logical_not(has_prev))
        def _():
            clear(0)

        @pl.when(has_next)
        def _():
            halo(False).wait_recv()
            spread_halo(rows + 1)

        @pl.when(jnp.logical_not(has_next))
        def _():
            clear(rows + 1)

    def send_halo():
        @pl.when(has_prev)
        def _():
            halo(False).start()

        @pl.when(has_next)
        def _():
            halo(True).start()

    whole.wait()

    @pl.loop(0, rows + LAG)
    def _(i):
        @pl.when(i < rows)
        def _():
            attend(order(i))

        j = i - LAG

        @pl.when(j >= 0)
        def _():
            activate(order(j))

        @pl.when(j == 1)
        def _():
            send_halo()

        @pl.when(j == 5)
        def _():
            finish_halo()

        @pl.when(j >= 3)
        def _():
            @pl.loop(0, jnp.where(j == 5, 2, 1))
            def _(second):
                convolve(jnp.where(second == 0, j - 2, 0))

    @pl.loop(rows - 2, rows)
    def _(r):
        convolve(r)

    @pl.loop(0, rows)
    def _(r):
        @pl.loop(1, n_dev)
        def _(k):
            forward(r, k).wait_send()
            backward(r, k).wait_send()

    @pl.when(has_prev)
    def _():
        halo(False).wait_send()

    @pl.when(has_next)
    def _():
        halo(True).wait_send()


def local(n_dev, n_strip, clip, w_query, w_key, w_value, w_out, w_conv, conv_bias):
    fl, rows, width, chans = clip.shape
    frames = fl * n_dev
    pw = width // n_dev
    sizes = (n_dev, n_strip, fl, rows, width, chans)
    bf16 = jnp.bfloat16
    vmem = pl.BlockSpec(memory_space=pltpu.VMEM)
    hbm = pl.BlockSpec(memory_space=pl.ANY)
    positions = fl * rows * width
    return pl.pallas_call(
        functools.partial(kernel, sizes),
        out_shape=pltpu.VMEM((fl, 2 * rows, width, chans // 2), bf16),
        in_specs=[hbm] + [vmem] * 6,
        out_specs=vmem,
        scratch_shapes=[
            pltpu.VMEM((fl, rows, width, chans), bf16),
            pltpu.VMEM((rows, frames, pw, chans), bf16),
            pltpu.VMEM((rows, frames, pw, chans), bf16),
            pltpu.VMEM((rows, fl, width, chans), bf16),
            pltpu.VMEM((rows + 2, fl, width, 3 * chans), bf16),
            pltpu.VMEM((2 * chans, chans), bf16),
            pltpu.SemaphoreType.DMA,
            pltpu.SemaphoreType.DMA((rows, n_dev)),
            pltpu.SemaphoreType.DMA((rows, n_dev)),
            pltpu.SemaphoreType.DMA((rows, n_dev)),
            pltpu.SemaphoreType.DMA((rows, n_dev)),
            pltpu.SemaphoreType.DMA((2,)),
            pltpu.SemaphoreType.DMA((2,)),
        ],
        compiler_params=pltpu.CompilerParams(
            collective_id=0, has_side_effects=True, vmem_limit_bytes=48 * 1024 * 1024
        ),
        cost_estimate=pl.CostEstimate(
            flops=positions * chans * chans * 2 * 13,
            bytes_accessed=positions * chans * 2 * 4,
            transcendentals=positions * chans * 8,
        ),
    )(
        clip, w_query, w_key, w_value, w_out,
        w_conv.reshape(3, 3 * chans, chans), conv_bias.reshape(1, chans),
    )


def solution(mesh):
    placed = (P("frames", "rows", None, None), P(), P(), P(), P(), P(), P())
    return jax.shard_map(
        functools.partial(local, mesh.shape["frames"], mesh.shape["rows"]),
        mesh=mesh,
        in_specs=placed,
        out_specs=P("frames", "rows", None, None),
        check_vma=False,
    )
```

```python
import functools
import math

import jax
import jax.numpy as jnp
from jax import lax
from jax.experimental import pallas as pl
from jax.experimental.pallas import tpu as pltpu
from jax.sharding import PartitionSpec as P

HEADS = 8
PAIRS = HEADS // 2
LAG = 4
MESH = pl.DeviceIdType.MESH
NT = (((1,), (1,)), ((), ()))


def attend_block(x, wqv_t, wk, wo):
    frames, pixels, chans = x.shape
    n = frames * 8
    groups = pixels // 8
    hd = chans // HEADS
    half = chans // 2
    x = x.astype(jnp.float32)
    mean = jnp.mean(x, axis=-1, keepdims=True)
    centred = x - mean
    var = jnp.mean(centred * centred, axis=-1, keepdims=True)
    xn = centred * lax.rsqrt(var + 1e-6)
    xs = jnp.concatenate(
        [xn[:, 8 * g:8 * g + 8].reshape(n, chans) for g in range(groups)], axis=0
    ).astype(jnp.bfloat16)
    qv = lax.dot_general(wqv_t, xs, NT, preferred_element_type=jnp.float32).astype(jnp.bfloat16)
    keys = jnp.dot(xs, wk, preferred_element_type=jnp.float32).astype(jnp.bfloat16)

    low = lax.broadcasted_iota(jnp.int32, (n, half), 1) < half // 2
    first = jnp.where(low, 1.0, 0.0).astype(jnp.bfloat16)
    second = jnp.where(low, 0.0, 1.0).astype(jnp.bfloat16)
    none = jnp.zeros((hd, n), jnp.bfloat16)
    own = lax.broadcasted_iota(jnp.int32, (8, 2 * n), 0) == (
        lax.broadcasted_iota(jnp.int32, (8, 2 * n), 1) & 7
    )
    scale = math.log2(math.e) / math.sqrt(hd)

    def scores(g):
        q_t, k = qv[:chans, g * n:(g + 1) * n], keys[g * n:(g + 1) * n]
        out = []
        for side in range(2):
            heads = [
                q_t[side * half + hd * h:side * half + hd * (h + 1)] for h in range(HEADS // 2)
            ]
            rhs = jnp.concatenate(
                [
                    jnp.concatenate([q if h % 2 == parity else none for h, q in enumerate(heads)], axis=0)
                    for parity in range(2)
                ],
                axis=1,
            )
            k_side = k[:, side * half:(side + 1) * half]
            lhs = jnp.concatenate([k_side * first, k_side * second], axis=0)
            out.append(jnp.dot(lhs, rhs, preferred_element_type=jnp.float32))
        return out

    def weigh(g, s):
        v_t = qv[chans:, g * n:(g + 1) * n]
        pieces = []
        for j in range(PAIRS):
            sj = s[j // 2][(j % 2) * n:(j % 2 + 1) * n].reshape(frames, 8, 2 * n)
            top = jnp.max(sj, axis=0, keepdims=True)
            e = jnp.exp2((sj - top) * scale)
            total = jnp.sum(e, axis=0)
            inv = jnp.where(own, 1.0 / total, 0.0)
            p = (e * inv[None]).reshape(n, 2 * n).astype(jnp.bfloat16)
            o = jnp.dot(v_t[2 * hd * j:2 * hd * (j + 1)], p, preferred_element_type=jnp.float32)
            pieces += [o[:hd, :n], o[hd:, n:]]
        return jnp.concatenate(pieces, axis=0).T

    attended = []
    ahead = scores(0)
    for g in range(groups):
        now = ahead
        if g + 1 < groups:
            ahead = scores(g + 1)
        attended.append(weigh(g, now))
    attended = jnp.concatenate(attended, axis=0).astype(jnp.bfloat16)
    out = jnp.dot(attended, wo, preferred_element_type=jnp.float32)
    return jnp.concatenate(
        [out[g * n:(g + 1) * n].reshape(frames, 8, chans) for g in range(groups)], axis=1
    ).astype(jnp.bfloat16)


def offsets(n_dev):
    chips = list(range(1, n_dev // 2))
    swapped = list(chips)
    for i in range(0, len(chips) - 1, 2):
        swapped[i], swapped[i + 1] = chips[i + 1], chips[i]
    return [[2 * chip + half for half in range(2) for chip in c] + [1] for c in (chips, swapped)]


def kernel(
    sizes, clip, wq_in, wk_in, wv_in, wo_in, wc_in, bias_in, out,
    clipv, xr, pr, back, act, part, wqv_t, wq, wk, wv, wo, wc, bias,
    clip_sem, w_sem, f_send, f_recv, b_send, b_recv, h_send, h_recv,
):
    n_dev, n_strip, fl, rows, width, chans = sizes
    pw = width // n_dev
    me = lax.axis_index("frames")
    strip = lax.axis_index("rows")
    mine = pl.multiple_of(me * pw, pw)

    def peer(k):
        out = 0
        for bit in range(n_dev.bit_length() - 1):
            one = 1 << bit
            out = out + lax.rem(lax.div(me, one) + lax.div(k, one), 2) * one
        return out

    def start_to_all(copy, r):
        core = lax.rem(me, 2)
        for a, b in zip(*offsets(n_dev)):
            copy(r, jnp.where(core == 0, a, b)).start()

    def forward(r, k):
        to = peer(k)
        return pltpu.make_async_remote_copy(
            src_ref=clip.at[:, r, pl.ds(pl.multiple_of(to * pw, pw), pw), :],
            dst_ref=xr.at[r, pl.ds(me * fl, fl)],
            send_sem=f_send.at[r, k],
            recv_sem=f_recv.at[r, k],
            device_id={"frames": to},
            device_id_type=MESH,
        )

    def forward_own(r):
        return pltpu.make_async_copy(
            clip.at[:, r, pl.ds(mine, pw), :], xr.at[r, pl.ds(me * fl, fl)], f_recv.at[r, 0]
        )

    def backward(r, k):
        to = peer(k)
        return pltpu.make_async_remote_copy(
            src_ref=pr.at[r, pl.ds(to * fl, fl)],
            dst_ref=back.at[r, :, pl.ds(mine, pw), :],
            send_sem=b_send.at[r, k],
            recv_sem=b_recv.at[r, k],
            device_id={"frames": to},
            device_id_type=MESH,
        )

    def backward_own(r):
        return pltpu.make_async_copy(
            pr.at[r, pl.ds(me * fl, fl)], back.at[r, :, pl.ds(mine, pw), :], b_recv.at[r, 0]
        )

    def halo(down):
        src, dst = (rows, 0) if down else (1, rows + 1)
        return pltpu.make_async_remote_copy(
            src_ref=act.at[src, :, :, pl.ds(chans, chans)],
            dst_ref=act.at[dst, :, :, pl.ds(chans, chans)],
            send_sem=h_send.at[int(down)],
            recv_sem=h_recv.at[int(down)],
            device_id={"rows": strip + 1 if down else strip - 1},
            device_id_type=MESH,
        )

    def order(i):
        return jnp.where(i == 0, 0, jnp.where(i == 1, rows - 1, i - 1))

    has_prev, has_next = strip > 0, strip < n_strip - 1

    weights = [
        pltpu.make_async_copy(src, dst, w_sem.at[i])
        for i, (src, dst) in enumerate(
            [(wq_in, wq), (wv_in, wv), (wk_in, wk), (wo_in, wo), (wc_in, wc), (bias_in, bias)]
        )
    ]

    barrier = pltpu.get_barrier_semaphore()

    @pl.loop(1, n_dev)
    def _(k):
        pl.semaphore_signal(barrier, inc=1, device_id={"frames": peer(k)}, device_id_type=MESH)

    @pl.when(has_prev)
    def _():
        pl.semaphore_signal(barrier, inc=1, device_id={"rows": strip - 1}, device_id_type=MESH)

    @pl.when(has_next)
    def _():
        pl.semaphore_signal(barrier, inc=1, device_id={"rows": strip + 1}, device_id_type=MESH)

    for copy in weights:
        copy.start()

    @pl.loop(0, rows)
    def _(i):
        forward_own(order(i)).start()

    pl.semaphore_wait(
        barrier, n_dev - 1 + has_prev.astype(jnp.int32) + has_next.astype(jnp.int32)
    )

    @pl.loop(0, rows)
    def _(i):
        start_to_all(forward, order(i))

    whole = pltpu.make_async_copy(clip, clipv, clip_sem)
    whole.start()
    for copy in weights:
        copy.wait()
    wqv_t[:chans] = wq[...].astype(jnp.float32).T.astype(jnp.bfloat16)
    wqv_t[chans:] = wv[...].astype(jnp.float32).T.astype(jnp.bfloat16)

    def attend(r):
        forward_own(r).wait()

        @pl.loop(1, n_dev)
        def _(k):
            forward(r, k).wait_recv()

        block = min(pw, 32)

        @pl.loop(0, pw // block)
        def _(b):
            at = pl.ds(pl.multiple_of(b * block, block), block)
            pr[r, :, at, :] = attend_block(xr[r, :, at, :], wqv_t[...], wk[...], wo[...])

        start_to_all(backward, r)
        backward_own(r).start()

    def spread(a, row, f):
        pixel = lax.broadcasted_iota(jnp.int32, a.shape, 0)
        before = jnp.where(pixel == 0, 0.0, pltpu.roll(a, 1, 0))
        after = jnp.where(pixel == width - 1, 0.0, pltpu.roll(a, width - 1, 0))
        act[row, f, :, pl.ds(0, chans)] = before.astype(jnp.bfloat16)
        act[row, f, :, pl.ds(2 * chans, chans)] = after.astype(jnp.bfloat16)

    def activate(r):
        backward_own(r).wait()

        @pl.loop(1, n_dev)
        def _(k):
            backward(r, k).wait_recv()

        @pl.loop(0, fl)
        def _(f):
            h = clipv[f, r].astype(jnp.float32) + back[r, f].astype(jnp.float32)
            half = 0.5 * h
            a = half + half * jnp.tanh(half)
            act[r + 1, f, :, pl.ds(chans, chans)] = a.astype(jnp.bfloat16)
            spread(a, r + 1, f)

    def tiles(body):
        tile = min(width, 256)

        @pl.loop(0, fl)
        def _(f):
            @pl.loop(0, width // tile)
            def _(t):
                body(f, pl.ds(pl.multiple_of(t * tile, tile), tile))

    def taps(r, d, f, at):
        return jnp.dot(act[r + d, f, at, :], wc[d], preferred_element_type=jnp.float32)

    def finish(r, f, at, convolved):
        hidden = clipv[f, r, at, :].astype(jnp.float32) + back[r, f, at, :].astype(jnp.float32)
        mixed = (hidden + convolved + bias[...]).astype(jnp.bfloat16)
        out[f, 2 * r, at, :] = mixed[:, :chans // 2]
        out[f, 2 * r + 1, at, :] = mixed[:, chans // 2:]

    def convolve(r):
        tiles(lambda f, at: finish(r, f, at, sum(taps(r, d, f, at) for d in range(3))))

    def begin_last(t):
        r = rows - 3 + t
        one, two = t // 2, 1 + (t + 1) // 2

        def body(f, at):
            part[t, f, at, :] = taps(r, one, f, at) + taps(r, two, f, at)

        tiles(body)

    def finish_last(t):
        r = rows - 3 + t
        tiles(lambda f, at: finish(r, f, at, part[t, f, at, :] + taps(r, 2 - t, f, at)))

    def spread_halo(row):
        @pl.loop(0, fl)
        def _(f):
            spread(act[row, f, :, pl.ds(chans, chans)].astype(jnp.float32), row, f)

    def clear(row):
        act[row] = jnp.zeros(act.shape[1:], act.dtype)

    def finish_halo():
        @pl.when(has_prev)
        def _():
            halo(True).wait_recv()
            spread_halo(0)

        @pl.when(jnp.logical_not(has_prev))
        def _():
            clear(0)

        @pl.when(has_next)
        def _():
            halo(False).wait_recv()
            spread_halo(rows + 1)

        @pl.when(jnp.logical_not(has_next))
        def _():
            clear(rows + 1)

    def send_halo():
        @pl.when(has_prev)
        def _():
            halo(False).start()

        @pl.when(has_next)
        def _():
            halo(True).start()

    whole.wait()

    @pl.loop(0, rows + LAG)
    def _(i):
        @pl.when(i < rows)
        def _():
            attend(order(i))

        j = i - LAG

        @pl.when(j == rows - 1)
        def _():
            @pl.loop(0, 3)
            def _(t):
                begin_last(t)

        @pl.when(j >= 0)
        def _():
            activate(order(j))

        @pl.when(j == 1)
        def _():
            send_halo()

        @pl.when(j == 5)
        def _():
            finish_halo()

        @pl.when(jnp.logical_and(j >= 3, j < rows - 1))
        def _():
            @pl.loop(0, jnp.where(j == 5, 2, 1))
            def _(second):
                convolve(jnp.where(second == 0, j - 2, 0))

    @pl.loop(0, 3)
    def _(t):
        finish_last(t)

    @pl.loop(0, rows)
    def _(r):
        @pl.loop(1, n_dev)
        def _(k):
            forward(r, k).wait_send()
            backward(r, k).wait_send()

    @pl.when(has_prev)
    def _():
        halo(False).wait_send()

    @pl.when(has_next)
    def _():
        halo(True).wait_send()


def local(n_dev, n_strip, clip, w_query, w_key, w_value, w_out, w_conv, conv_bias):
    fl, rows, width, chans = clip.shape
    frames = fl * n_dev
    pw = width // n_dev
    sizes = (n_dev, n_strip, fl, rows, width, chans)
    bf16 = jnp.bfloat16
    vmem = pl.BlockSpec(memory_space=pltpu.VMEM)
    hbm = pl.BlockSpec(memory_space=pltpu.HBM)
    positions = fl * rows * width
    return pl.pallas_call(
        functools.partial(kernel, sizes),
        out_shape=pltpu.VMEM((fl, 2 * rows, width, chans // 2), bf16),
        in_specs=[hbm] * 7,
        out_specs=vmem,
        scratch_shapes=[
            pltpu.VMEM((fl, rows, width, chans), bf16),
            pltpu.VMEM((rows, frames, pw, chans), bf16),
            pltpu.VMEM((rows, frames, pw, chans), bf16),
            pltpu.VMEM((rows, fl, width, chans), bf16),
            pltpu.VMEM((rows + 2, fl, width, 3 * chans), bf16),
            pltpu.VMEM((3, fl, width, chans), jnp.float32),
            pltpu.VMEM((2 * chans, chans), bf16),
            pltpu.VMEM((chans, chans), bf16),
            pltpu.VMEM((chans, chans), bf16),
            pltpu.VMEM((chans, chans), bf16),
            pltpu.VMEM((chans, chans), bf16),
            pltpu.VMEM((3, 3 * chans, chans), bf16),
            pltpu.VMEM((1, chans), jnp.float32),
            pltpu.SemaphoreType.DMA,
            pltpu.SemaphoreType.DMA((6,)),
            pltpu.SemaphoreType.DMA((rows, n_dev)),
            pltpu.SemaphoreType.DMA((rows, n_dev)),
            pltpu.SemaphoreType.DMA((rows, n_dev)),
            pltpu.SemaphoreType.DMA((rows, n_dev)),
            pltpu.SemaphoreType.DMA((2,)),
            pltpu.SemaphoreType.DMA((2,)),
        ],
        compiler_params=pltpu.CompilerParams(
            collective_id=0, has_side_effects=True, vmem_limit_bytes=59 * 1024 * 1024
        ),
        cost_estimate=pl.CostEstimate(
            flops=positions * chans * chans * 2 * 13,
            bytes_accessed=positions * chans * 2 * 4,
            transcendentals=positions * chans * 8,
        ),
    )(
        clip, w_query, w_key, w_value, w_out,
        w_conv.reshape(3, 3 * chans, chans), conv_bias.reshape(1, chans),
    )


def solution(mesh):
    placed = (P("frames", "rows", None, None), P(), P(), P(), P(), P(), P())
    return jax.shard_map(
        functools.partial(local, mesh.shape["frames"], mesh.shape["rows"]),
        mesh=mesh,
        in_specs=placed,
        out_specs=P("frames", "rows", None, None),
        check_vma=False,
    )
```

```python
import functools
import math

import jax
import jax.numpy as jnp
from jax import lax
from jax.experimental import pallas as pl
from jax.experimental.pallas import tpu as pltpu
from jax.sharding import PartitionSpec as P

HEADS = 8
PAIRS = HEADS // 2
LAG = 4
MESH = pl.DeviceIdType.MESH
NT = (((1,), (1,)), ((), ()))


def attend_block(x, wqv_t, wk, wo):
    frames, pixels, chans = x.shape
    n = frames * 8
    groups = pixels // 8
    hd = chans // HEADS
    half = chans // 2
    x = x.astype(jnp.float32)
    mean = jnp.mean(x, axis=-1, keepdims=True)
    centred = x - mean
    var = jnp.mean(centred * centred, axis=-1, keepdims=True)
    xn = centred * lax.rsqrt(var + 1e-6)
    xs = jnp.concatenate(
        [xn[:, 8 * g:8 * g + 8].reshape(n, chans) for g in range(groups)], axis=0
    ).astype(jnp.bfloat16)
    qv = lax.dot_general(wqv_t, xs, NT, preferred_element_type=jnp.float32).astype(jnp.bfloat16)
    keys = jnp.dot(xs, wk, preferred_element_type=jnp.float32).astype(jnp.bfloat16)

    low = lax.broadcasted_iota(jnp.int32, (n, half), 1) < half // 2
    first = jnp.where(low, 1.0, 0.0).astype(jnp.bfloat16)
    second = jnp.where(low, 0.0, 1.0).astype(jnp.bfloat16)
    none = jnp.zeros((hd, n), jnp.bfloat16)
    own = lax.broadcasted_iota(jnp.int32, (8, 2 * n), 0) == (
        lax.broadcasted_iota(jnp.int32, (8, 2 * n), 1) & 7
    )
    scale = math.log2(math.e) / math.sqrt(hd)

    def scores(g):
        q_t, k = qv[:chans, g * n:(g + 1) * n], keys[g * n:(g + 1) * n]
        out = []
        for side in range(2):
            heads = [
                q_t[side * half + hd * h:side * half + hd * (h + 1)] for h in range(HEADS // 2)
            ]
            rhs = jnp.concatenate(
                [
                    jnp.concatenate([q if h % 2 == parity else none for h, q in enumerate(heads)], axis=0)
                    for parity in range(2)
                ],
                axis=1,
            )
            k_side = k[:, side * half:(side + 1) * half]
            lhs = jnp.concatenate([k_side * first, k_side * second], axis=0)
            out.append(jnp.dot(lhs, rhs, preferred_element_type=jnp.float32))
        return out

    def weigh(g, s):
        v_t = qv[chans:, g * n:(g + 1) * n]
        pieces = []
        for j in range(PAIRS):
            sj = s[j // 2][(j % 2) * n:(j % 2 + 1) * n].reshape(frames, 8, 2 * n)
            top = jnp.max(sj, axis=0, keepdims=True)
            e = jnp.exp2((sj - top) * scale)
            total = jnp.sum(e, axis=0)
            inv = jnp.where(own, 1.0 / total, 0.0)
            p = (e * inv[None]).reshape(n, 2 * n).astype(jnp.bfloat16)
            o = jnp.dot(v_t[2 * hd * j:2 * hd * (j + 1)], p, preferred_element_type=jnp.float32)
            pieces += [o[:hd, :n], o[hd:, n:]]
        return jnp.concatenate(pieces, axis=0).T

    attended = []
    ahead = scores(0)
    for g in range(groups):
        now = ahead
        if g + 1 < groups:
            ahead = scores(g + 1)
        attended.append(weigh(g, now))
    attended = jnp.concatenate(attended, axis=0).astype(jnp.bfloat16)
    out = jnp.dot(attended, wo, preferred_element_type=jnp.float32)
    return jnp.concatenate(
        [out[g * n:(g + 1) * n].reshape(frames, 8, chans) for g in range(groups)], axis=1
    ).astype(jnp.bfloat16)


def offsets(n_dev):
    chips = list(range(1, n_dev // 2))
    swapped = list(chips)
    for i in range(0, len(chips) - 1, 2):
        swapped[i], swapped[i + 1] = chips[i + 1], chips[i]
    return [[2 * chip + half for half in range(2) for chip in c] + [1] for c in (chips, swapped)]


def kernel(
    sizes, clip, wq_in, wk_in, wv_in, wo_in, wc_in, bias_in, out,
    clipv, xr, pr, back, act, part, wqv_t, wq, wk, wv, wo, wc, bias,
    clip_sem, w_sem, f_send, f_recv, b_send, b_recv, l_send, l_recv, h_send, h_recv,
):
    n_dev, n_strip, fl, rows, width, chans = sizes
    pw = width // n_dev
    me = lax.axis_index("frames")
    strip = lax.axis_index("rows")
    mine = pl.multiple_of(me * pw, pw)

    def peer(k):
        out = 0
        for bit in range(n_dev.bit_length() - 1):
            one = 1 << bit
            out = out + lax.rem(lax.div(me, one) + lax.div(k, one), 2) * one
        return out

    def start_to_all(copy, r):
        core = lax.rem(me, 2)
        for a, b in zip(*offsets(n_dev)):
            copy(r, jnp.where(core == 0, a, b)).start()

    def forward(r, k):
        to = peer(k)
        return pltpu.make_async_remote_copy(
            src_ref=clip.at[:, r, pl.ds(pl.multiple_of(to * pw, pw), pw), :],
            dst_ref=xr.at[r, pl.ds(me * fl, fl)],
            send_sem=f_send.at[r, k],
            recv_sem=f_recv.at[r, k],
            device_id={"frames": to},
            device_id_type=MESH,
        )

    def forward_own(r):
        return pltpu.make_async_copy(
            clip.at[:, r, pl.ds(mine, pw), :], xr.at[r, pl.ds(me * fl, fl)], f_recv.at[r, 0]
        )

    def backward(r, k):
        to = peer(k)
        return pltpu.make_async_remote_copy(
            src_ref=pr.at[r, pl.ds(to * fl, fl)],
            dst_ref=back.at[r, :, pl.ds(mine, pw), :],
            send_sem=b_send.at[r, k],
            recv_sem=b_recv.at[r, k],
            device_id={"frames": to},
            device_id_type=MESH,
        )

    def backward_own(r):
        return pltpu.make_async_copy(
            pr.at[r, pl.ds(me * fl, fl)], back.at[r, :, pl.ds(mine, pw), :], b_recv.at[r, 0]
        )

    last = rows - 2

    def backward_frame(f, k):
        to = peer(k)
        return pltpu.make_async_remote_copy(
            src_ref=pr.at[last, to * fl + f],
            dst_ref=back.at[last, f, pl.ds(mine, pw), :],
            send_sem=l_send.at[f, k],
            recv_sem=l_recv.at[f, k],
            device_id={"frames": to},
            device_id_type=MESH,
        )

    def wait_sent(copy, r):
        @pl.loop(1, n_dev)
        def _(k):
            copy(r, k).wait_send()

    def halo(down):
        src, dst = (rows, 0) if down else (1, rows + 1)
        return pltpu.make_async_remote_copy(
            src_ref=act.at[src, :, :, pl.ds(chans, chans)],
            dst_ref=act.at[dst, :, :, pl.ds(chans, chans)],
            send_sem=h_send.at[int(down)],
            recv_sem=h_recv.at[int(down)],
            device_id={"rows": strip + 1 if down else strip - 1},
            device_id_type=MESH,
        )

    def order(i):
        return jnp.where(i == 0, 0, jnp.where(i == 1, rows - 1, i - 1))

    has_prev, has_next = strip > 0, strip < n_strip - 1

    weights = [
        pltpu.make_async_copy(src, dst, w_sem.at[i])
        for i, (src, dst) in enumerate(
            [(wq_in, wq), (wv_in, wv), (wk_in, wk), (wo_in, wo), (wc_in, wc), (bias_in, bias)]
        )
    ]

    barrier = pltpu.get_barrier_semaphore()

    @pl.loop(1, n_dev)
    def _(k):
        pl.semaphore_signal(barrier, inc=1, device_id={"frames": peer(k)}, device_id_type=MESH)

    @pl.when(has_prev)
    def _():
        pl.semaphore_signal(barrier, inc=1, device_id={"rows": strip - 1}, device_id_type=MESH)

    @pl.when(has_next)
    def _():
        pl.semaphore_signal(barrier, inc=1, device_id={"rows": strip + 1}, device_id_type=MESH)

    for copy in weights:
        copy.start()

    @pl.loop(0, rows)
    def _(i):
        forward_own(order(i)).start()

    pl.semaphore_wait(
        barrier, n_dev - 1 + has_prev.astype(jnp.int32) + has_next.astype(jnp.int32)
    )

    @pl.loop(0, rows)
    def _(i):
        start_to_all(forward, order(i))

    whole = pltpu.make_async_copy(clip, clipv, clip_sem)
    whole.start()
    for copy in weights:
        copy.wait()
    wqv_t[:chans] = wq[...].astype(jnp.float32).T.astype(jnp.bfloat16)
    wqv_t[chans:] = wv[...].astype(jnp.float32).T.astype(jnp.bfloat16)

    def attend(r):
        forward_own(r).wait()

        @pl.loop(1, n_dev)
        def _(k):
            forward(r, k).wait_recv()

        block = min(pw, 32)

        @pl.loop(0, pw // block)
        def _(b):
            at = pl.ds(pl.multiple_of(b * block, block), block)
            pr[r, :, at, :] = attend_block(xr[r, :, at, :], wqv_t[...], wk[...], wo[...])

        backward_own(r).start()

        @pl.when(r != last)
        def _():
            start_to_all(backward, r)

        @pl.when(r == last)
        def _():
            @pl.loop(0, fl)
            def _(f):
                start_to_all(backward_frame, f)

    def spread(a, row, f):
        pixel = lax.broadcasted_iota(jnp.int32, a.shape, 0)
        before = jnp.where(pixel == 0, 0.0, pltpu.roll(a, 1, 0))
        after = jnp.where(pixel == width - 1, 0.0, pltpu.roll(a, width - 1, 0))
        act[row, f, :, pl.ds(0, chans)] = before.astype(jnp.bfloat16)
        act[row, f, :, pl.ds(2 * chans, chans)] = after.astype(jnp.bfloat16)

    def activate_frame(r, f):
        h = clipv[f, r].astype(jnp.float32) + back[r, f].astype(jnp.float32)
        half = 0.5 * h
        a = half + half * jnp.tanh(half)
        act[r + 1, f, :, pl.ds(chans, chans)] = a.astype(jnp.bfloat16)
        spread(a, r + 1, f)

    def activate(r):
        backward_own(r).wait()

        @pl.loop(1, n_dev)
        def _(k):
            backward(r, k).wait_recv()

        @pl.loop(0, fl)
        def _(f):
            activate_frame(r, f)

    def frame_tiles(f, body):
        tile = min(width, 256)

        @pl.loop(0, width // tile)
        def _(t):
            body(f, pl.ds(pl.multiple_of(t * tile, tile), tile))

    def tiles(body):
        @pl.loop(0, fl)
        def _(f):
            frame_tiles(f, body)

    def taps(r, d, f, at):
        return jnp.dot(act[r + d, f, at, :], wc[d], preferred_element_type=jnp.float32)

    def finish(r, f, at, convolved):
        hidden = clipv[f, r, at, :].astype(jnp.float32) + back[r, f, at, :].astype(jnp.float32)
        mixed = (hidden + convolved + bias[...]).astype(jnp.bfloat16)
        out[f, 2 * r, at, :] = mixed[:, :chans // 2]
        out[f, 2 * r + 1, at, :] = mixed[:, chans // 2:]

    def convolve(r):
        tiles(lambda f, at: finish(r, f, at, sum(taps(r, d, f, at) for d in range(3))))

    def begin_last(t):
        r = rows - 3 + t
        one, two = t // 2, 1 + (t + 1) // 2

        def body(f, at):
            part[t, f, at, :] = taps(r, one, f, at) + taps(r, two, f, at)

        tiles(body)

    def finish_last(t, f):
        r = rows - 3 + t
        frame_tiles(f, lambda f, at: finish(r, f, at, part[t, f, at, :] + taps(r, 2 - t, f, at)))

    def spread_halo(row):
        @pl.loop(0, fl)
        def _(f):
            spread(act[row, f, :, pl.ds(chans, chans)].astype(jnp.float32), row, f)

    def clear(row):
        act[row] = jnp.zeros(act.shape[1:], act.dtype)

    def finish_halo():
        @pl.when(has_prev)
        def _():
            halo(True).wait_recv()
            spread_halo(0)

        @pl.when(jnp.logical_not(has_prev))
        def _():
            clear(0)

        @pl.when(has_next)
        def _():
            halo(False).wait_recv()
            spread_halo(rows + 1)

        @pl.when(jnp.logical_not(has_next))
        def _():
            clear(rows + 1)

    def send_halo():
        @pl.when(has_prev)
        def _():
            halo(False).start()

        @pl.when(has_next)
        def _():
            halo(True).start()

    whole.wait()

    @pl.loop(0, rows - 1 + LAG)
    def _(i):
        @pl.when(i < rows)
        def _():
            attend(order(i))

        j = i - LAG

        @pl.when(j >= 0)
        def _():
            activate(order(j))
            wait_sent(forward, order(j))

        @pl.when(j == 1)
        def _():
            send_halo()

        @pl.when(j >= 2)
        def _():
            wait_sent(backward, order(j - 2))

        @pl.when(j == 5)
        def _():
            finish_halo()

        @pl.when(j >= 3)
        def _():
            @pl.loop(0, jnp.where(j == 5, 2, 1))
            def _(second):
                convolve(jnp.where(second == 0, j - 2, 0))

    @pl.loop(0, 3)
    def _(t):
        begin_last(t)

    @pl.loop(rows - 3, rows - 1)
    def _(j):
        wait_sent(backward, order(j))

    wait_sent(forward, last)

    @pl.when(has_prev)
    def _():
        halo(False).wait_send()

    @pl.when(has_next)
    def _():
        halo(True).wait_send()

    backward_own(last).wait()

    @pl.loop(0, fl)
    def _(f):
        @pl.loop(1, n_dev)
        def _(k):
            backward_frame(f, k).wait_recv()

        activate_frame(last, f)

        @pl.loop(0, 3)
        def _(t):
            finish_last(t, f)

    @pl.loop(0, fl)
    def _(f):
        wait_sent(backward_frame, f)


def local(n_dev, n_strip, clip, w_query, w_key, w_value, w_out, w_conv, conv_bias):
    fl, rows, width, chans = clip.shape
    frames = fl * n_dev
    pw = width // n_dev
    sizes = (n_dev, n_strip, fl, rows, width, chans)
    bf16 = jnp.bfloat16
    vmem = pl.BlockSpec(memory_space=pltpu.VMEM)
    hbm = pl.BlockSpec(memory_space=pltpu.HBM)
    positions = fl * rows * width
    return pl.pallas_call(
        functools.partial(kernel, sizes),
        out_shape=pltpu.VMEM((fl, 2 * rows, width, chans // 2), bf16),
        in_specs=[hbm] * 7,
        out_specs=vmem,
        scratch_shapes=[
            pltpu.VMEM((fl, rows, width, chans), bf16),
            pltpu.VMEM((rows, frames, pw, chans), bf16),
            pltpu.VMEM((rows, frames, pw, chans), bf16),
            pltpu.VMEM((rows, fl, width, chans), bf16),
            pltpu.VMEM((rows + 2, fl, width, 3 * chans), bf16),
            pltpu.VMEM((3, fl, width, chans), jnp.float32),
            pltpu.VMEM((2 * chans, chans), bf16),
            pltpu.VMEM((chans, chans), bf16),
            pltpu.VMEM((chans, chans), bf16),
            pltpu.VMEM((chans, chans), bf16),
            pltpu.VMEM((chans, chans), bf16),
            pltpu.VMEM((3, 3 * chans, chans), bf16),
            pltpu.VMEM((1, chans), jnp.float32),
            pltpu.SemaphoreType.DMA,
            pltpu.SemaphoreType.DMA((6,)),
            pltpu.SemaphoreType.DMA((rows, n_dev)),
            pltpu.SemaphoreType.DMA((rows, n_dev)),
            pltpu.SemaphoreType.DMA((rows, n_dev)),
            pltpu.SemaphoreType.DMA((rows, n_dev)),
            pltpu.SemaphoreType.DMA((fl, n_dev)),
            pltpu.SemaphoreType.DMA((fl, n_dev)),
            pltpu.SemaphoreType.DMA((2,)),
            pltpu.SemaphoreType.DMA((2,)),
        ],
        compiler_params=pltpu.CompilerParams(
            collective_id=0, has_side_effects=True, vmem_limit_bytes=59 * 1024 * 1024
        ),
        cost_estimate=pl.CostEstimate(
            flops=positions * chans * chans * 2 * 13,
            bytes_accessed=positions * chans * 2 * 4,
            transcendentals=positions * chans * 8,
        ),
    )(
        clip, w_query, w_key, w_value, w_out,
        w_conv.reshape(3, 3 * chans, chans), conv_bias.reshape(1, chans),
    )


def solution(mesh):
    placed = (P("frames", "rows", None, None), P(), P(), P(), P(), P(), P())
    return jax.shard_map(
        functools.partial(local, mesh.shape["frames"], mesh.shape["rows"]),
        mesh=mesh,
        in_specs=placed,
        out_specs=P("frames", "rows", None, None),
        check_vma=False,
    )
```

```python
import functools
import math

import jax
import jax.numpy as jnp
from jax import lax
from jax.experimental import pallas as pl
from jax.experimental.pallas import tpu as pltpu
from jax.sharding import PartitionSpec as P

HEADS = 8
LAG = 4
MESH = pl.DeviceIdType.MESH
NT = (((1,), (1,)), ((), ()))


def attend_block(x, wqv_t, wk, wo):
    frames, pixels, chans = x.shape
    n = frames * 8
    groups = pixels // 8
    hd = chans // HEADS
    half = chans // 2
    x = x.astype(jnp.float32)
    mean = jnp.mean(x, axis=-1, keepdims=True)
    centred = x - mean
    var = jnp.mean(centred * centred, axis=-1, keepdims=True)
    xn = centred * lax.rsqrt(var + 1e-6)
    xs = jnp.concatenate(
        [xn[:, 8 * g:8 * g + 8].reshape(n, chans) for g in range(groups)], axis=0
    ).astype(jnp.bfloat16)
    qv = lax.dot_general(wqv_t, xs, NT, preferred_element_type=jnp.float32).astype(jnp.bfloat16)
    keys = jnp.dot(xs, wk, preferred_element_type=jnp.float32).astype(jnp.bfloat16)

    low = lax.broadcasted_iota(jnp.int32, (n, half), 1) < half // 2
    first = jnp.where(low, 1.0, 0.0).astype(jnp.bfloat16)
    second = jnp.where(low, 0.0, 1.0).astype(jnp.bfloat16)
    none = jnp.zeros((hd, n), jnp.bfloat16)
    own = lax.broadcasted_iota(jnp.int32, (8, 2 * n), 0) == (
        lax.broadcasted_iota(jnp.int32, (8, 2 * n), 1) & 7
    )
    scale = math.log2(math.e) / math.sqrt(hd)

    def scores(g):
        q_t, k = qv[:chans, g * n:(g + 1) * n], keys[g * n:(g + 1) * n]
        out = []
        for side in range(2):
            heads = [
                q_t[side * half + hd * h:side * half + hd * (h + 1)] for h in range(HEADS // 2)
            ]
            rhs = jnp.concatenate(
                [
                    jnp.concatenate([q if h % 2 == parity else none for h, q in enumerate(heads)], axis=0)
                    for parity in range(2)
                ],
                axis=1,
            )
            k_side = k[:, side * half:(side + 1) * half]
            lhs = jnp.concatenate([k_side * first, k_side * second], axis=0)
            out.append(jnp.dot(lhs, rhs, preferred_element_type=jnp.float32))
        return out

    def probabilities(s):
        s = s.reshape(2, frames, 8, 2 * n)
        top = jnp.max(s, axis=1, keepdims=True)
        e = jnp.exp2((s - top) * scale)
        inv = jnp.where(own, 1.0 / jnp.sum(e, axis=1), 0.0)
        return (e * inv[:, None]).reshape(2 * n, 2 * n).astype(jnp.bfloat16)

    gap = jnp.zeros((2 * hd, n), jnp.bfloat16)

    def weigh(g, side, p):
        v_t = qv[chans + side * half:chans + (side + 1) * half, g * n:(g + 1) * n]
        values = jnp.concatenate(
            [
                jnp.concatenate([v_t[:2 * hd], gap], axis=1),
                jnp.concatenate([gap, v_t[2 * hd:]], axis=1),
            ],
            axis=0,
        )
        o = jnp.dot(values, p, preferred_element_type=jnp.float32)
        return [
            o[hd * h:hd * (h + 1), (h % 2) * n:(h % 2 + 1) * n] for h in range(HEADS // 2)
        ]

    everything = [scores(g) for g in range(groups)]
    probs = [[probabilities(s) for s in sides] for sides in everything]
    heads = [
        weigh(g, 0, probs[g][0]) + weigh(g, 1, probs[g][1]) for g in range(groups)
    ]
    attended = [jnp.concatenate(h, axis=0).T for h in heads]
    attended = jnp.concatenate(attended, axis=0).astype(jnp.bfloat16)
    out = jnp.dot(attended, wo, preferred_element_type=jnp.float32)
    return jnp.concatenate(
        [out[g * n:(g + 1) * n].reshape(frames, 8, chans) for g in range(groups)], axis=1
    ).astype(jnp.bfloat16)


def offsets(n_dev):
    chips = list(range(1, n_dev // 2))
    swapped = list(chips)
    for i in range(0, len(chips) - 1, 2):
        swapped[i], swapped[i + 1] = chips[i + 1], chips[i]
    return [[2 * chip + half for half in range(2) for chip in c] + [1] for c in (chips, swapped)]


def kernel(
    sizes, clip, wq_in, wk_in, wv_in, wo_in, wc_in, bias_in, out,
    clipv, xr, pr, back, act, part, wqv_t, wq, wk, wv, wo, wc, bias,
    clip_sem, w_sem, f_send, f_recv, b_send, b_recv, l_send, l_recv, h_send, h_recv,
):
    n_dev, n_strip, fl, rows, width, chans = sizes
    pw = width // n_dev
    me = lax.axis_index("frames")
    strip = lax.axis_index("rows")
    mine = pl.multiple_of(me * pw, pw)

    def peer(k):
        out = 0
        for bit in range(n_dev.bit_length() - 1):
            one = 1 << bit
            out = out + lax.rem(lax.div(me, one) + lax.div(k, one), 2) * one
        return out

    def start_to_all(copy, r):
        core = lax.rem(me, 2)
        for a, b in zip(*offsets(n_dev)):
            copy(r, jnp.where(core == 0, a, b)).start()

    def forward(r, k):
        to = peer(k)
        return pltpu.make_async_remote_copy(
            src_ref=clip.at[:, r, pl.ds(pl.multiple_of(to * pw, pw), pw), :],
            dst_ref=xr.at[r, pl.ds(me * fl, fl)],
            send_sem=f_send.at[r, k],
            recv_sem=f_recv.at[r, k],
            device_id={"frames": to},
            device_id_type=MESH,
        )

    def forward_own(r):
        return pltpu.make_async_copy(
            clip.at[:, r, pl.ds(mine, pw), :], xr.at[r, pl.ds(me * fl, fl)], f_recv.at[r, 0]
        )

    def backward(r, k):
        to = peer(k)
        return pltpu.make_async_remote_copy(
            src_ref=pr.at[r, pl.ds(to * fl, fl)],
            dst_ref=back.at[r, :, pl.ds(mine, pw), :],
            send_sem=b_send.at[r, k],
            recv_sem=b_recv.at[r, k],
            device_id={"frames": to},
            device_id_type=MESH,
        )

    def backward_own(r):
        return pltpu.make_async_copy(
            pr.at[r, pl.ds(me * fl, fl)], back.at[r, :, pl.ds(mine, pw), :], b_recv.at[r, 0]
        )

    last = rows - 2

    def backward_frame(f, k):
        to = peer(k)
        return pltpu.make_async_remote_copy(
            src_ref=pr.at[last, to * fl + f],
            dst_ref=back.at[last, f, pl.ds(mine, pw), :],
            send_sem=l_send.at[f, k],
            recv_sem=l_recv.at[f, k],
            device_id={"frames": to},
            device_id_type=MESH,
        )

    def wait_sent(copy, r):
        @pl.loop(1, n_dev)
        def _(k):
            copy(r, k).wait_send()

    def halo(down):
        src, dst = (rows, 0) if down else (1, rows + 1)
        return pltpu.make_async_remote_copy(
            src_ref=act.at[src, :, :, pl.ds(chans, chans)],
            dst_ref=act.at[dst, :, :, pl.ds(chans, chans)],
            send_sem=h_send.at[int(down)],
            recv_sem=h_recv.at[int(down)],
            device_id={"rows": strip + 1 if down else strip - 1},
            device_id_type=MESH,
        )

    def order(i):
        return jnp.where(i == 0, 0, jnp.where(i == 1, rows - 1, i - 1))

    has_prev, has_next = strip > 0, strip < n_strip - 1

    weights = [
        pltpu.make_async_copy(src, dst, w_sem.at[i])
        for i, (src, dst) in enumerate(
            [(wq_in, wq), (wv_in, wv), (wk_in, wk), (wo_in, wo), (wc_in, wc), (bias_in, bias)]
        )
    ]

    barrier = pltpu.get_barrier_semaphore()

    @pl.loop(1, n_dev)
    def _(k):
        pl.semaphore_signal(barrier, inc=1, device_id={"frames": peer(k)}, device_id_type=MESH)

    @pl.when(has_prev)
    def _():
        pl.semaphore_signal(barrier, inc=1, device_id={"rows": strip - 1}, device_id_type=MESH)

    @pl.when(has_next)
    def _():
        pl.semaphore_signal(barrier, inc=1, device_id={"rows": strip + 1}, device_id_type=MESH)

    for copy in weights:
        copy.start()

    @pl.loop(0, rows)
    def _(i):
        forward_own(order(i)).start()

    pl.semaphore_wait(
        barrier, n_dev - 1 + has_prev.astype(jnp.int32) + has_next.astype(jnp.int32)
    )

    @pl.loop(0, rows)
    def _(i):
        start_to_all(forward, order(i))

    whole = pltpu.make_async_copy(clip, clipv, clip_sem)
    whole.start()
    for copy in weights:
        copy.wait()
    wqv_t[:chans] = wq[...].astype(jnp.float32).T.astype(jnp.bfloat16)
    wqv_t[chans:] = wv[...].astype(jnp.float32).T.astype(jnp.bfloat16)

    def attend(r):
        forward_own(r).wait()

        @pl.loop(1, n_dev)
        def _(k):
            forward(r, k).wait_recv()

        block = min(pw, 32)

        @pl.loop(0, pw // block)
        def _(b):
            at = pl.ds(pl.multiple_of(b * block, block), block)
            pr[r, :, at, :] = attend_block(xr[r, :, at, :], wqv_t[...], wk[...], wo[...])

        backward_own(r).start()

        @pl.when(r != last)
        def _():
            start_to_all(backward, r)

        @pl.when(r == last)
        def _():
            @pl.loop(0, fl)
            def _(f):
                start_to_all(backward_frame, f)

    def spread(a, row, f):
        pixel = lax.broadcasted_iota(jnp.int32, a.shape, 0)
        before = jnp.where(pixel == 0, 0.0, pltpu.roll(a, 1, 0))
        after = jnp.where(pixel == width - 1, 0.0, pltpu.roll(a, width - 1, 0))
        act[row, f, :, pl.ds(0, chans)] = before.astype(jnp.bfloat16)
        act[row, f, :, pl.ds(2 * chans, chans)] = after.astype(jnp.bfloat16)

    def activate_frame(r, f):
        h = clipv[f, r].astype(jnp.float32) + back[r, f].astype(jnp.float32)
        half = 0.5 * h
        a = half + half * jnp.tanh(half)
        act[r + 1, f, :, pl.ds(chans, chans)] = a.astype(jnp.bfloat16)
        spread(a, r + 1, f)

    def activate(r):
        backward_own(r).wait()

        @pl.loop(1, n_dev)
        def _(k):
            backward(r, k).wait_recv()

        @pl.loop(0, fl)
        def _(f):
            activate_frame(r, f)

    def frame_tiles(f, body):
        tile = min(width, 512)

        @pl.loop(0, width // tile)
        def _(t):
            body(f, pl.ds(pl.multiple_of(t * tile, tile), tile))

    def tiles(body):
        @pl.loop(0, fl)
        def _(f):
            frame_tiles(f, body)

    def taps(r, d, f, at):
        return jnp.dot(act[r + d, f, at, :], wc[d], preferred_element_type=jnp.float32)

    def finish(r, f, at, convolved):
        hidden = clipv[f, r, at, :].astype(jnp.float32) + back[r, f, at, :].astype(jnp.float32)
        mixed = (hidden + convolved + bias[...]).astype(jnp.bfloat16)
        out[f, 2 * r, at, :] = mixed[:, :chans // 2]
        out[f, 2 * r + 1, at, :] = mixed[:, chans // 2:]

    def convolve(r):
        tiles(lambda f, at: finish(r, f, at, sum(taps(r, d, f, at) for d in range(3))))

    def begin_last(t):
        r = rows - 3 + t
        one, two = t // 2, 1 + (t + 1) // 2

        def body(f, at):
            part[t, f, at, :] = taps(r, one, f, at) + taps(r, two, f, at)

        tiles(body)

    def finish_last(t, f):
        r = rows - 3 + t
        frame_tiles(f, lambda f, at: finish(r, f, at, part[t, f, at, :] + taps(r, 2 - t, f, at)))

    def spread_halo(row):
        @pl.loop(0, fl)
        def _(f):
            spread(act[row, f, :, pl.ds(chans, chans)].astype(jnp.float32), row, f)

    def clear(row):
        act[row] = jnp.zeros(act.shape[1:], act.dtype)

    def finish_halo():
        @pl.when(has_prev)
        def _():
            halo(True).wait_recv()
            spread_halo(0)

        @pl.when(jnp.logical_not(has_prev))
        def _():
            clear(0)

        @pl.when(has_next)
        def _():
            halo(False).wait_recv()
            spread_halo(rows + 1)

        @pl.when(jnp.logical_not(has_next))
        def _():
            clear(rows + 1)

    def send_halo():
        @pl.when(has_prev)
        def _():
            halo(False).start()

        @pl.when(has_next)
        def _():
            halo(True).start()

    whole.wait()

    @pl.loop(0, rows - 1 + LAG)
    def _(i):
        @pl.when(i < rows)
        def _():
            attend(order(i))

        j = i - LAG

        @pl.when(j >= 0)
        def _():
            activate(order(j))
            wait_sent(forward, order(j))

        @pl.when(j == 1)
        def _():
            send_halo()

        @pl.when(j >= 2)
        def _():
            wait_sent(backward, order(j - 2))

        @pl.when(j == 5)
        def _():
            finish_halo()

        @pl.when(j >= 3)
        def _():
            @pl.loop(0, jnp.where(j == 5, 2, 1))
            def _(second):
                convolve(jnp.where(second == 0, j - 2, 0))

    @pl.loop(0, 3)
    def _(t):
        begin_last(t)

    @pl.loop(rows - 3, rows - 1)
    def _(j):
        wait_sent(backward, order(j))

    wait_sent(forward, last)

    @pl.when(has_prev)
    def _():
        halo(False).wait_send()

    @pl.when(has_next)
    def _():
        halo(True).wait_send()

    backward_own(last).wait()

    @pl.loop(0, fl)
    def _(f):
        @pl.loop(1, n_dev)
        def _(k):
            backward_frame(f, k).wait_recv()

        activate_frame(last, f)

        @pl.loop(0, 3)
        def _(t):
            finish_last(t, f)

    @pl.loop(0, fl)
    def _(f):
        wait_sent(backward_frame, f)


def local(n_dev, n_strip, clip, w_query, w_key, w_value, w_out, w_conv, conv_bias):
    fl, rows, width, chans = clip.shape
    frames = fl * n_dev
    pw = width // n_dev
    sizes = (n_dev, n_strip, fl, rows, width, chans)
    bf16 = jnp.bfloat16
    vmem = pl.BlockSpec(memory_space=pltpu.VMEM)
    hbm = pl.BlockSpec(memory_space=pltpu.HBM)
    positions = fl * rows * width
    return pl.pallas_call(
        functools.partial(kernel, sizes),
        out_shape=pltpu.VMEM((fl, 2 * rows, width, chans // 2), bf16),
        in_specs=[hbm] * 7,
        out_specs=vmem,
        scratch_shapes=[
            pltpu.VMEM((fl, rows, width, chans), bf16),
            pltpu.VMEM((rows, frames, pw, chans), bf16),
            pltpu.VMEM((rows, frames, pw, chans), bf16),
            pltpu.VMEM((rows, fl, width, chans), bf16),
            pltpu.VMEM((rows + 2, fl, width, 3 * chans), bf16),
            pltpu.VMEM((3, fl, width, chans), jnp.float32),
            pltpu.VMEM((2 * chans, chans), bf16),
            pltpu.VMEM((chans, chans), bf16),
            pltpu.VMEM((chans, chans), bf16),
            pltpu.VMEM((chans, chans), bf16),
            pltpu.VMEM((chans, chans), bf16),
            pltpu.VMEM((3, 3 * chans, chans), bf16),
            pltpu.VMEM((1, chans), jnp.float32),
            pltpu.SemaphoreType.DMA,
            pltpu.SemaphoreType.DMA((6,)),
            pltpu.SemaphoreType.DMA((rows, n_dev)),
            pltpu.SemaphoreType.DMA((rows, n_dev)),
            pltpu.SemaphoreType.DMA((rows, n_dev)),
            pltpu.SemaphoreType.DMA((rows, n_dev)),
            pltpu.SemaphoreType.DMA((fl, n_dev)),
            pltpu.SemaphoreType.DMA((fl, n_dev)),
            pltpu.SemaphoreType.DMA((2,)),
            pltpu.SemaphoreType.DMA((2,)),
        ],
        compiler_params=pltpu.CompilerParams(
            collective_id=0, has_side_effects=True, vmem_limit_bytes=59 * 1024 * 1024
        ),
        cost_estimate=pl.CostEstimate(
            flops=positions * chans * chans * 2 * 13,
            bytes_accessed=positions * chans * 2 * 4,
            transcendentals=positions * chans * 8,
        ),
    )(
        clip, w_query, w_key, w_value, w_out,
        w_conv.reshape(3, 3 * chans, chans), conv_bias.reshape(1, chans),
    )


def solution(mesh):
    placed = (P("frames", "rows", None, None), P(), P(), P(), P(), P(), P())
    return jax.shard_map(
        functools.partial(local, mesh.shape["frames"], mesh.shape["rows"]),
        mesh=mesh,
        in_specs=placed,
        out_specs=P("frames", "rows", None, None),
        check_vma=False,
    )
```

```python
import functools
import math

import jax
import jax.numpy as jnp
from jax import lax
from jax.experimental import pallas as pl
from jax.experimental.pallas import tpu as pltpu
from jax.sharding import PartitionSpec as P

HEADS = 8
LAG = 4
MESH = pl.DeviceIdType.MESH
NT = (((1,), (1,)), ((), ()))


def attend_block(x, wqv_t, wk, wo):
    frames, pixels, chans = x.shape
    n = frames * 8
    groups = pixels // 8
    hd = chans // HEADS
    half = chans // 2
    x = x.astype(jnp.float32)
    mean = jnp.mean(x, axis=-1, keepdims=True)
    centred = x - mean
    var = jnp.mean(centred * centred, axis=-1, keepdims=True)
    xn = centred * lax.rsqrt(var + 1e-6)
    xs = jnp.concatenate(
        [xn[:, 8 * g:8 * g + 8].reshape(n, chans) for g in range(groups)], axis=0
    ).astype(jnp.bfloat16)
    qv = lax.dot_general(wqv_t, xs, NT, preferred_element_type=jnp.float32).astype(jnp.bfloat16)
    keys = jnp.dot(xs, wk, preferred_element_type=jnp.float32).astype(jnp.bfloat16)

    low = lax.broadcasted_iota(jnp.int32, (n, half), 1) < half // 2
    first = jnp.where(low, 1.0, 0.0).astype(jnp.bfloat16)
    second = jnp.where(low, 0.0, 1.0).astype(jnp.bfloat16)
    none = jnp.zeros((hd, n), jnp.bfloat16)
    own = lax.broadcasted_iota(jnp.int32, (8, 2 * n), 0) == (
        lax.broadcasted_iota(jnp.int32, (8, 2 * n), 1) & 7
    )
    scale = math.log2(math.e) / math.sqrt(hd)

    def scores(g):
        q_t, k = qv[:chans, g * n:(g + 1) * n], keys[g * n:(g + 1) * n]
        out = []
        for side in range(2):
            heads = [
                q_t[side * half + hd * h:side * half + hd * (h + 1)] for h in range(HEADS // 2)
            ]
            rhs = jnp.concatenate(
                [
                    jnp.concatenate([q if h % 2 == parity else none for h, q in enumerate(heads)], axis=0)
                    for parity in range(2)
                ],
                axis=1,
            )
            k_side = k[:, side * half:(side + 1) * half]
            lhs = jnp.concatenate([k_side * first, k_side * second], axis=0)
            out.append(jnp.dot(lhs, rhs, preferred_element_type=jnp.float32))
        return out

    def probabilities(s):
        s = s.reshape(2, frames, 8, 2 * n)
        top = jnp.max(s, axis=1, keepdims=True)
        e = jnp.exp2((s - top) * scale)
        inv = jnp.where(own, 1.0 / jnp.sum(e, axis=1), 0.0)
        return (e * inv[:, None]).reshape(2 * n, 2 * n).astype(jnp.bfloat16)

    gap = jnp.zeros((2 * hd, n), jnp.bfloat16)

    def weigh(g, side, p):
        v_t = qv[chans + side * half:chans + (side + 1) * half, g * n:(g + 1) * n]
        values = jnp.concatenate(
            [
                jnp.concatenate([v_t[:2 * hd], gap], axis=1),
                jnp.concatenate([gap, v_t[2 * hd:]], axis=1),
            ],
            axis=0,
        )
        o = jnp.dot(values, p, preferred_element_type=jnp.float32)
        return [
            o[hd * h:hd * (h + 1), (h % 2) * n:(h % 2 + 1) * n] for h in range(HEADS // 2)
        ]

    everything = [scores(g) for g in range(groups)]
    probs = [[probabilities(s) for s in sides] for sides in everything]
    heads = [
        weigh(g, 0, probs[g][0]) + weigh(g, 1, probs[g][1]) for g in range(groups)
    ]
    attended = [jnp.concatenate(h, axis=0).T for h in heads]
    attended = jnp.concatenate(attended, axis=0).astype(jnp.bfloat16)
    out = jnp.dot(attended, wo, preferred_element_type=jnp.float32)
    return jnp.concatenate(
        [out[g * n:(g + 1) * n].reshape(frames, 8, chans) for g in range(groups)], axis=1
    ).astype(jnp.bfloat16)


def offsets(n_dev):
    chips = list(range(1, n_dev // 2))
    swapped = list(chips)
    for i in range(0, len(chips) - 1, 2):
        swapped[i], swapped[i + 1] = chips[i + 1], chips[i]
    return [[2 * chip + half for half in range(2) for chip in c] + [1] for c in (chips, swapped)]


def kernel(
    sizes, clip, wq_in, wk_in, wv_in, wo_in, wc_in, bias_in, out,
    clipv, xr, pr, back, act, part, wqv_t, wq, wk, wv, wo, wc, bias,
    clip_sem, w_sem, f_send, f_recv, b_send, b_recv, l_send, l_recv, h_send, h_recv,
):
    n_dev, n_strip, fl, rows, width, chans = sizes
    pw = width // n_dev
    me = lax.axis_index("frames")
    strip = lax.axis_index("rows")
    mine = pl.multiple_of(me * pw, pw)

    def peer(k):
        out = 0
        for bit in range(n_dev.bit_length() - 1):
            one = 1 << bit
            out = out + lax.rem(lax.div(me, one) + lax.div(k, one), 2) * one
        return out

    def start_to_all(copy, r):
        core = lax.rem(me, 2)
        for a, b in zip(*offsets(n_dev)):
            copy(r, jnp.where(core == 0, a, b)).start()

    def forward(r, k):
        to = peer(k)
        return pltpu.make_async_remote_copy(
            src_ref=clip.at[:, r, pl.ds(pl.multiple_of(to * pw, pw), pw), :],
            dst_ref=xr.at[r, pl.ds(me * fl, fl)],
            send_sem=f_send.at[r, k],
            recv_sem=f_recv.at[r, k],
            device_id={"frames": to},
            device_id_type=MESH,
        )

    def forward_own(r):
        return pltpu.make_async_copy(
            clip.at[:, r, pl.ds(mine, pw), :], xr.at[r, pl.ds(me * fl, fl)], f_recv.at[r, 0]
        )

    def backward(r, k):
        to = peer(k)
        return pltpu.make_async_remote_copy(
            src_ref=pr.at[r, pl.ds(to * fl, fl)],
            dst_ref=back.at[r, :, pl.ds(mine, pw), :],
            send_sem=b_send.at[r, k],
            recv_sem=b_recv.at[r, k],
            device_id={"frames": to},
            device_id_type=MESH,
        )

    def backward_own(r):
        return pltpu.make_async_copy(
            pr.at[r, pl.ds(me * fl, fl)], back.at[r, :, pl.ds(mine, pw), :], b_recv.at[r, 0]
        )

    last = rows - 2

    def backward_frame(f, k):
        to = peer(k)
        return pltpu.make_async_remote_copy(
            src_ref=pr.at[last, to * fl + f],
            dst_ref=back.at[last, f, pl.ds(mine, pw), :],
            send_sem=l_send.at[f, k],
            recv_sem=l_recv.at[f, k],
            device_id={"frames": to},
            device_id_type=MESH,
        )

    def wait_sent(copy, r):
        @pl.loop(1, n_dev)
        def _(k):
            copy(r, k).wait_send()

    def halo(down):
        src, dst = (rows, 0) if down else (1, rows + 1)
        return pltpu.make_async_remote_copy(
            src_ref=act.at[src, :, :, pl.ds(chans, chans)],
            dst_ref=act.at[dst, :, :, pl.ds(chans, chans)],
            send_sem=h_send.at[int(down)],
            recv_sem=h_recv.at[int(down)],
            device_id={"rows": strip + 1 if down else strip - 1},
            device_id_type=MESH,
        )

    def order(i):
        return jnp.where(i == 0, 0, jnp.where(i == 1, rows - 1, i - 1))

    has_prev, has_next = strip > 0, strip < n_strip - 1

    weights = [
        pltpu.make_async_copy(src, dst, w_sem.at[i])
        for i, (src, dst) in enumerate(
            [(wq_in, wq), (wv_in, wv), (wk_in, wk), (wo_in, wo), (wc_in, wc), (bias_in, bias)]
        )
    ]

    barrier = pltpu.get_barrier_semaphore()

    @pl.loop(1, n_dev)
    def _(k):
        pl.semaphore_signal(barrier, inc=1, device_id={"frames": peer(k)}, device_id_type=MESH)

    @pl.when(has_prev)
    def _():
        pl.semaphore_signal(barrier, inc=1, device_id={"rows": strip - 1}, device_id_type=MESH)

    @pl.when(has_next)
    def _():
        pl.semaphore_signal(barrier, inc=1, device_id={"rows": strip + 1}, device_id_type=MESH)

    whole = pltpu.make_async_copy(clip, clipv, clip_sem)
    whole.start()
    for copy in weights:
        copy.start()

    @pl.loop(0, rows)
    def _(i):
        forward_own(order(i)).start()

    pl.semaphore_wait(
        barrier, n_dev - 1 + has_prev.astype(jnp.int32) + has_next.astype(jnp.int32)
    )

    @pl.loop(0, rows)
    def _(i):
        start_to_all(forward, order(i))

    for copy in weights:
        copy.wait()
    wqv_t[:chans] = wq[...].astype(jnp.float32).T.astype(jnp.bfloat16)
    wqv_t[chans:] = wv[...].astype(jnp.float32).T.astype(jnp.bfloat16)

    def attend(r):
        forward_own(r).wait()

        @pl.loop(1, n_dev)
        def _(k):
            forward(r, k).wait_recv()

        block = min(pw, 32)

        @pl.loop(0, pw // block)
        def _(b):
            at = pl.ds(pl.multiple_of(b * block, block), block)
            pr[r, :, at, :] = attend_block(xr[r, :, at, :], wqv_t[...], wk[...], wo[...])

        backward_own(r).start()

        @pl.when(r != last)
        def _():
            start_to_all(backward, r)

        @pl.when(r == last)
        def _():
            @pl.loop(0, fl)
            def _(f):
                start_to_all(backward_frame, f)

    def spread(a, row, f):
        pixel = lax.broadcasted_iota(jnp.int32, a.shape, 0)
        before = jnp.where(pixel == 0, 0.0, pltpu.roll(a, 1, 0))
        after = jnp.where(pixel == width - 1, 0.0, pltpu.roll(a, width - 1, 0))
        act[row, f, :, pl.ds(0, chans)] = before.astype(jnp.bfloat16)
        act[row, f, :, pl.ds(2 * chans, chans)] = after.astype(jnp.bfloat16)

    def activate_frame(r, f):
        h = clipv[f, r].astype(jnp.float32) + back[r, f].astype(jnp.float32)
        half = 0.5 * h
        a = half + half * jnp.tanh(half)
        act[r + 1, f, :, pl.ds(chans, chans)] = a.astype(jnp.bfloat16)
        spread(a, r + 1, f)

    def activate(r):
        backward_own(r).wait()

        @pl.loop(1, n_dev)
        def _(k):
            backward(r, k).wait_recv()

        @pl.loop(0, fl)
        def _(f):
            activate_frame(r, f)

    def frame_tiles(f, body):
        tile = min(width, 512)

        @pl.loop(0, width // tile)
        def _(t):
            body(f, pl.ds(pl.multiple_of(t * tile, tile), tile))

    def tiles(body):
        @pl.loop(0, fl)
        def _(f):
            frame_tiles(f, body)

    def taps(r, d, f, at):
        return jnp.dot(act[r + d, f, at, :], wc[d], preferred_element_type=jnp.float32)

    def finish(r, f, at, convolved):
        hidden = clipv[f, r, at, :].astype(jnp.float32) + back[r, f, at, :].astype(jnp.float32)
        mixed = (hidden + convolved + bias[...]).astype(jnp.bfloat16)
        out[f, 2 * r, at, :] = mixed[:, :chans // 2]
        out[f, 2 * r + 1, at, :] = mixed[:, chans // 2:]

    def convolve(r):
        tiles(lambda f, at: finish(r, f, at, sum(taps(r, d, f, at) for d in range(3))))

    def begin_last(t):
        r = rows - 3 + t
        one, two = t // 2, 1 + (t + 1) // 2

        def body(f, at):
            part[t, f, at, :] = taps(r, one, f, at) + taps(r, two, f, at)

        tiles(body)

    def finish_last(t, f):
        r = rows - 3 + t
        frame_tiles(f, lambda f, at: finish(r, f, at, part[t, f, at, :] + taps(r, 2 - t, f, at)))

    def spread_halo(row):
        @pl.loop(0, fl)
        def _(f):
            spread(act[row, f, :, pl.ds(chans, chans)].astype(jnp.float32), row, f)

    def clear(row):
        act[row] = jnp.zeros(act.shape[1:], act.dtype)

    def finish_halo():
        @pl.when(has_prev)
        def _():
            halo(True).wait_recv()
            spread_halo(0)

        @pl.when(jnp.logical_not(has_prev))
        def _():
            clear(0)

        @pl.when(has_next)
        def _():
            halo(False).wait_recv()
            spread_halo(rows + 1)

        @pl.when(jnp.logical_not(has_next))
        def _():
            clear(rows + 1)

    def send_halo():
        @pl.when(has_prev)
        def _():
            halo(False).start()

        @pl.when(has_next)
        def _():
            halo(True).start()

    @pl.loop(0, rows - 1 + LAG)
    def _(i):
        @pl.when(i < rows)
        def _():
            attend(order(i))

        j = i - LAG

        @pl.when(j == 0)
        def _():
            whole.wait()

        @pl.when(j >= 0)
        def _():
            activate(order(j))
            wait_sent(forward, order(j))

        @pl.when(j == 1)
        def _():
            send_halo()

        @pl.when(j >= 2)
        def _():
            wait_sent(backward, order(j - 2))

        @pl.when(j == 5)
        def _():
            finish_halo()

        @pl.when(j >= 3)
        def _():
            @pl.loop(0, jnp.where(j == 5, 2, 1))
            def _(second):
                convolve(jnp.where(second == 0, j - 2, 0))

    @pl.loop(0, 3)
    def _(t):
        begin_last(t)

    @pl.loop(rows - 3, rows - 1)
    def _(j):
        wait_sent(backward, order(j))

    wait_sent(forward, last)

    @pl.when(has_prev)
    def _():
        halo(False).wait_send()

    @pl.when(has_next)
    def _():
        halo(True).wait_send()

    backward_own(last).wait()

    @pl.loop(0, fl)
    def _(f):
        @pl.loop(1, n_dev)
        def _(k):
            backward_frame(f, k).wait_recv()

        activate_frame(last, f)

        @pl.loop(0, 3)
        def _(t):
            finish_last(t, f)

    @pl.loop(0, fl)
    def _(f):
        wait_sent(backward_frame, f)


def local(n_dev, n_strip, clip, w_query, w_key, w_value, w_out, w_conv, conv_bias):
    fl, rows, width, chans = clip.shape
    frames = fl * n_dev
    pw = width // n_dev
    sizes = (n_dev, n_strip, fl, rows, width, chans)
    bf16 = jnp.bfloat16
    vmem = pl.BlockSpec(memory_space=pltpu.VMEM)
    hbm = pl.BlockSpec(memory_space=pltpu.HBM)
    positions = fl * rows * width
    return pl.pallas_call(
        functools.partial(kernel, sizes),
        out_shape=pltpu.VMEM((fl, 2 * rows, width, chans // 2), bf16),
        in_specs=[hbm] * 7,
        out_specs=vmem,
        scratch_shapes=[
            pltpu.VMEM((fl, rows, width, chans), bf16),
            pltpu.VMEM((rows, frames, pw, chans), bf16),
            pltpu.VMEM((rows, frames, pw, chans), bf16),
            pltpu.VMEM((rows, fl, width, chans), bf16),
            pltpu.VMEM((rows + 2, fl, width, 3 * chans), bf16),
            pltpu.VMEM((3, fl, width, chans), jnp.float32),
            pltpu.VMEM((2 * chans, chans), bf16),
            pltpu.VMEM((chans, chans), bf16),
            pltpu.VMEM((chans, chans), bf16),
            pltpu.VMEM((chans, chans), bf16),
            pltpu.VMEM((chans, chans), bf16),
            pltpu.VMEM((3, 3 * chans, chans), bf16),
            pltpu.VMEM((1, chans), jnp.float32),
            pltpu.SemaphoreType.DMA,
            pltpu.SemaphoreType.DMA((6,)),
            pltpu.SemaphoreType.DMA((rows, n_dev)),
            pltpu.SemaphoreType.DMA((rows, n_dev)),
            pltpu.SemaphoreType.DMA((rows, n_dev)),
            pltpu.SemaphoreType.DMA((rows, n_dev)),
            pltpu.SemaphoreType.DMA((fl, n_dev)),
            pltpu.SemaphoreType.DMA((fl, n_dev)),
            pltpu.SemaphoreType.DMA((2,)),
            pltpu.SemaphoreType.DMA((2,)),
        ],
        compiler_params=pltpu.CompilerParams(
            collective_id=0, has_side_effects=True, vmem_limit_bytes=59 * 1024 * 1024
        ),
        cost_estimate=pl.CostEstimate(
            flops=positions * chans * chans * 2 * 13,
            bytes_accessed=positions * chans * 2 * 4,
            transcendentals=positions * chans * 8,
        ),
    )(
        clip, w_query, w_key, w_value, w_out,
        w_conv.reshape(3, 3 * chans, chans), conv_bias.reshape(1, chans),
    )


def solution(mesh):
    placed = (P("frames", "rows", None, None), P(), P(), P(), P(), P(), P())
    return jax.shard_map(
        functools.partial(local, mesh.shape["frames"], mesh.shape["rows"]),
        mesh=mesh,
        in_specs=placed,
        out_specs=P("frames", "rows", None, None),
        check_vma=False,
    )
```
